128 devices in a mesh: section: 2 (over core), node: 64 (over x, z, y).
Axes of the slice: x: 4, y: 4, z: 4, core: 2. Of those that a mesh axis runs over, the one named last changes fastest.
Arguments:
- node_latents: bfloat16 [2, 16384, 512], P(None, 'node'), may hold values from -6 to 6
- edge_latents: bfloat16 [2, 98304, 512], P(None, 'node'), may hold values from -6 to 6
- sender: int32 [98304], P('node'), may hold values from 0 to 511
- receiver: int32 [98304], P('node'), may hold values from 0 to 255
- send_up: int32 [8192], P('node'), may hold values from 0 to 255
- send_down: int32 [8192], P('node'), may hold values from 0 to 255
- edge_count: int32 [64], P('node'), may hold values from 512 to 1536, as said below
- w_edge_in: bfloat16 [4, 1536, 512], P('section'), may hold values from -0.15625 to 0.15625
- w_edge_out: bfloat16 [4, 512, 512], P('section'), may hold values from -0.25 to 0.25
- edge_gain: float32 [4, 512], P('section'), may hold values from 0.25 to 1.75
- w_node_in: bfloat16 [4, 1024, 512], P('section'), may hold values from -0.1875 to 0.1875
- w_node_out: bfloat16 [4, 512, 512], P('section'), may hold values from -0.25 to 0.25
- node_gain: float32 [4, 512], P('section'), may hold values from 0.25 to 1.75
Outputs:
- processed: bfloat16 [2, 16384, 512], P('section', 'node')
The draws below stay inside these ranges and needn't reach their ends.
Inputs may be any that keep to these rules, and one draw needn't show every extreme that they name: `edge_count`: each shard has between 512 and 1536 live edge slots, and some shard has all 1536 live.
All inputs are finite; a program needn't handle non-finite values.
Results may differ from the reference program's by a relative error of at most 0.025.
Values may be sent and summed in bfloat16 or wider, within the bound.
A program may use at most 128 MiB of HBM per device.

```python
import jax
import jax.numpy as jnp
from jax import lax

D = 512
NV_DEV = 256
HALO = 128
EDGES_DEV = 1536
LAYERS = 4
MICRO = 2
NODES = 16384
EDGES = 98304
N_NODE = 64


def draw_edge_count(key, part):
    key = jax.random.fold_in(key, 11)
    first, second = jax.random.split(key)
    counts = jax.random.randint(first, (N_NODE,), EDGES_DEV // 3, EDGES_DEV + 1).astype(jnp.int32)
    fullest = jax.random.randint(second, (), 0, N_NODE)
    return counts.at[fullest].set(EDGES_DEV).astype(jnp.int32)


def set_ends(result, rng, smallest, largest):
    longest = result.shape.index(max(result.shape))
    spots = []
    for shift in (0, 1):
        where = [jax.random.randint(jax.random.fold_in(rng, axis), (), 0, length) for axis, length in enumerate(result.shape)]
        where[longest] = (where[longest] + shift) % result.shape[longest]
        spots.append(tuple(where))
    return result.at[spots[0]].set(smallest).at[spots[1]].set(largest)


def level_of(key, shape, shards, smallest, top_value):
    def one(dim, parts):
        steps = jax.random.uniform(jax.random.fold_in(jax.random.fold_in(key, 6), dim), (parts,), jnp.float32, smallest / len(shards), top_value / len(shards))
        return jnp.repeat(jnp.exp(steps), shape[dim] // parts).reshape((-1,) + (1,) * (len(shape) - dim - 1))

    factor_of = one(*shards[0])
    for cut in shards[1:]:
        factor_of = factor_of * one(*cut)
    return factor_of


def bell_draw(rng, dims, deviation, bound, shards=(), kind=jnp.bfloat16):
    array = deviation * jax.random.normal(rng, dims, jnp.float32)
    if shards:
        array = array * level_of(rng, dims, shards, -0.22, 0.18)
    return jnp.clip(array, -bound, bound).astype(kind)


def setup_inputs(seed: int = 0) -> dict:
    key_of = jax.random.split(jax.random.key(seed), 14)
    node_latents = bell_draw(key_of[0], (MICRO, NODES, D), 1.0, 6.0, ((1, 64),))
    edge_latents = bell_draw(key_of[1], (MICRO, EDGES, D), 1.0, 6.0, ((1, 64),))
    sender = set_ends(jax.random.randint(key_of[2], (EDGES,), 0, NV_DEV + 2 * HALO), jax.random.fold_in(key_of[2], 1), 0, (NV_DEV + 2 * HALO) - 1).astype(jnp.int32)
    receiver = set_ends(jax.random.randint(key_of[3], (EDGES,), 0, NV_DEV), jax.random.fold_in(key_of[3], 1), 0, NV_DEV - 1).astype(jnp.int32)
    send_up = set_ends(jax.random.randint(key_of[4], (HALO * N_NODE,), 0, NV_DEV), jax.random.fold_in(key_of[4], 1), 0, NV_DEV - 1).astype(jnp.int32)
    send_down = set_ends(jax.random.randint(key_of[5], (HALO * N_NODE,), 0, NV_DEV), jax.random.fold_in(key_of[5], 1), 0, NV_DEV - 1).astype(jnp.int32)
    edge_count = draw_edge_count(jax.random.fold_in(key_of[13], 71), 0)
    w_edge_in = bell_draw(key_of[7], (LAYERS, 3 * D, D), (3 * D) ** -0.5, 0.15625, ((0, 2),))
    w_edge_out = bell_draw(key_of[8], (LAYERS, D, D), D ** -0.5, 0.25, ((0, 2),))
    edge_gain = jnp.clip(1.0 + 0.15 * jax.random.normal(key_of[9], (LAYERS, D), jnp.float32), 0.25, 1.75)
    w_node_in = bell_draw(key_of[10], (LAYERS, 2 * D, D), (2 * D) ** -0.5, 0.1875, ((0, 2),))
    w_node_out = bell_draw(key_of[11], (LAYERS, D, D), D ** -0.5, 0.25, ((0, 2),))
    node_gain = jnp.clip(1.0 + 0.15 * jax.random.normal(key_of[12], (LAYERS, D), jnp.float32), 0.25, 1.75)
    return {"node_latents": node_latents, "edge_latents": edge_latents, "sender": sender, "receiver": receiver, "send_up": send_up, "send_down": send_down, "edge_count": edge_count, "w_edge_in": w_edge_in, "w_edge_out": w_edge_out, "edge_gain": edge_gain, "w_node_in": w_node_in, "w_node_out": w_node_out, "node_gain": node_gain}


def normed(values):
    mean = lax.optimization_barrier(jnp.mean(values, axis=-1, keepdims=True))
    var = lax.optimization_barrier(jnp.mean((values - mean) ** 2, axis=-1, keepdims=True))
    return (values - mean) * lax.rsqrt(var + 1e-05)

def one_layer(nodes, edges, table, sender, receiver, valid, w_in, w_out, e_gain, n_in, n_out, n_gain):
    width = nodes.shape[1]
    senders = jnp.take(table, sender, axis=0)
    receivers = jnp.take(nodes, receiver, axis=0)
    pre = jnp.dot(edges, w_in[:width], preferred_element_type=jnp.float32)
    pre = pre + jnp.dot(senders, w_in[width:2 * width], preferred_element_type=jnp.float32)
    pre = pre + jnp.dot(receivers, w_in[2 * width:], preferred_element_type=jnp.float32)
    hidden = jax.nn.silu(pre).astype(jnp.bfloat16)
    update = jnp.dot(hidden, w_out, preferred_element_type=jnp.float32)
    new_edges = (edges.astype(jnp.float32) + e_gain * normed(update)).astype(jnp.bfloat16)
    rows = jnp.arange(nodes.shape[0], dtype=jnp.int32)
    onehot = ((receiver[None, :] == rows[:, None]) & valid[None, :]).astype(jnp.bfloat16)
    aggregate = jnp.dot(onehot, new_edges, preferred_element_type=jnp.float32).astype(jnp.bfloat16)
    pre_node = jnp.dot(nodes, n_in[:width], preferred_element_type=jnp.float32)
    pre_node = pre_node + jnp.dot(aggregate, n_in[width:], preferred_element_type=jnp.float32)
    node_hidden = jax.nn.silu(pre_node).astype(jnp.bfloat16)
    node_update = jnp.dot(node_hidden, n_out, preferred_element_type=jnp.float32)
    new_nodes = (nodes.astype(jnp.float32) + n_gain * normed(node_update)).astype(jnp.bfloat16)
    return (new_nodes, new_edges)

def reference(node_latents, edge_latents, sender, receiver, send_up, send_down, edge_count, w_edge_in, w_edge_out, edge_gain, w_node_in, w_node_out, node_gain):
    width = node_latents.shape[2]
    senders_dev = sender.reshape(N_NODE, EDGES_DEV)
    receivers_dev = receiver.reshape(N_NODE, EDGES_DEV)
    up_dev = send_up.reshape(N_NODE, HALO)
    down_dev = send_down.reshape(N_NODE, HALO)
    slots = jnp.arange(EDGES_DEV, dtype=jnp.int32)
    valid_dev = slots[None, :] < edge_count[:, None]
    results = []
    for micro in range(MICRO):
        nodes = node_latents[micro].reshape(N_NODE, NV_DEV, width)
        edges = edge_latents[micro].reshape(N_NODE, EDGES_DEV, width)
        for layer in range(LAYERS):
            upward = jax.vmap(lambda block, index: jnp.take(block, index, axis=0))(nodes, up_dev)
            downward = jax.vmap(lambda block, index: jnp.take(block, index, axis=0))(nodes, down_dev)
            tables = jnp.concatenate([nodes, jnp.roll(upward, 1, axis=0), jnp.roll(downward, -1, axis=0)], axis=1)

            def per_shard(items, layer=layer):
                n_block, e_block, t_block, s_block, r_block, v_block = items
                return one_layer(n_block, e_block, t_block, s_block, r_block, v_block, w_edge_in[layer], w_edge_out[layer], edge_gain[layer], w_node_in[layer], w_node_out[layer], node_gain[layer])
            nodes, edges = lax.map(per_shard, (nodes, edges, tables, senders_dev, receivers_dev, valid_dev))
        results.append(nodes.reshape(NODES, width))
    return jnp.stack(results, axis=0)
```

```python
import functools

import jax
import jax.numpy as jnp
from jax import lax
from jax.experimental import pallas as pl
from jax.experimental.pallas import tpu as pltpu
from jax.sharding import PartitionSpec as P

D = 512
NV = 256
HALO = 128
E = 1536
L = 4
OWN = 2
TILE = 256
CHUNK = 128
MESH = pl.DeviceIdType.MESH

REC = D
LOC = REC + NV
HAL = LOC + NV
XW = HAL + 2 * HALO


def silu(x):
    half = 0.5 * x
    return half + half * jnp.tanh(half)


def residual_norm(base, update, gain):
    mean = jnp.mean(update, axis=-1, keepdims=True)
    centred = update - mean
    var = jnp.mean(centred * centred, axis=-1, keepdims=True)
    return (base.astype(jnp.float32) + gain * (centred * lax.rsqrt(var + 1e-05))).astype(jnp.bfloat16)


def dot(a, b):
    return jnp.dot(a, b, preferred_element_type=jnp.float32)


def kernel(
    n_node,
    node_in,
    edge_in,
    snd,
    rcv,
    upw,
    dnw,
    count,
    wei,
    weo,
    eg,
    wni,
    wno,
    ng,
    out,
    nodes,
    x,
    pre,
    oht,
    pick,
    wcat,
    w23,
    wo,
    ni,
    no,
    egs,
    ngs,
    halo,
    sendbuf,
    pre_node,
    in_sem,
    w_sem,
    ws_sem,
    h_recv,
    h_send,
):
    me = lax.axis_index("section")
    other = 1 - me
    at = lax.axis_index("node")
    above = lax.rem(at + 1, n_node)
    below = lax.rem(at + n_node - 1, n_node)

    copy_nodes = pltpu.make_async_copy(node_in.at[me], nodes, in_sem.at[0])
    copy_nodes.start()

    def pieces(j):
        k = OWN * me + j
        return [
            (wei.at[j, pl.ds(D, 2 * D)], w23.at[k]),
            (wei.at[j, pl.ds(0, D)], wcat.at[k, pl.ds(0, D)]),
            (weo.at[j], wo.at[k]),
            (wni.at[j], ni.at[k]),
            (wno.at[j], no.at[k]),
        ]

    own = []
    for j in range(OWN):
        for p, (src, dst) in enumerate(pieces(j)):
            own.append(pltpu.make_async_copy(src, dst, w_sem.at[OWN * me + j, p]))
    own.append(pltpu.make_async_copy(eg, egs.at[me], w_sem.at[me, 5]))
    own.append(pltpu.make_async_copy(ng, ngs.at[me], w_sem.at[me, 6]))
    for c in own[:5]:
        c.start()
    copy_edges = pltpu.make_async_copy(edge_in.at[me], x.at[:, pl.ds(0, D)], in_sem.at[1])
    copy_edges.start()
    for c in own[5:]:
        c.start()

    barrier = pltpu.get_barrier_semaphore()
    for target in ({"section": other}, {"node": above}, {"node": below}):
        pl.semaphore_signal(barrier, inc=1, device_id=target, device_id_type=MESH)
    pl.semaphore_wait(barrier, 3)

    remote = []
    for j in range(OWN):
        for p, (src, dst) in enumerate(pieces(j)):
            remote.append((src, dst, ws_sem.at[j, p], w_sem.at[OWN * me + j, p]))
    remote.insert(3, (eg, egs.at[me], ws_sem.at[0, 5], w_sem.at[me, 5]))
    remote.insert(4, (ng, ngs.at[me], ws_sem.at[0, 6], w_sem.at[me, 6]))
    remote = [
        pltpu.make_async_remote_copy(
            src_ref=s, dst_ref=d, send_sem=a, recv_sem=b, device_id={"section": other}, device_id_type=MESH
        )
        for s, d, a, b in remote
    ]
    for c in remote:
        c.start()

    def column(ref, k):
        return jnp.broadcast_to(ref[k : k + 1, :], (CHUNK, CHUNK)).T

    def hot(col, width, base):
        rows = col.shape[0]
        parts = []
        for q in range(width // CHUNK):
            lanes = lax.broadcasted_iota(jnp.int32, (rows, CHUNK), 1) + (base + q * CHUNK)
            parts.append(jnp.where(col == lanes, 1.0, 0.0).astype(jnp.bfloat16))
        return jnp.concatenate(parts, axis=1)

    pick[pl.ds(0, HALO), :] = hot(column(upw, 0), NV, 0)
    pick[pl.ds(HALO, HALO), :] = hot(column(dnw, 0), NV, 0)

    def halo_copies(l):
        return [
            pltpu.make_async_remote_copy(
                src_ref=sendbuf.at[l, pl.ds(q * HALO, HALO)],
                dst_ref=halo.at[l, pl.ds(q * HALO, HALO)],
                send_sem=h_send.at[l, q],
                recv_sem=h_recv.at[l, q],
                device_id={"node": target},
                device_id_type=MESH,
            )
            for q, target in enumerate((above, below))
        ]

    def send_halo(l):
        sendbuf[l] = dot(pick[...], nodes[...]).astype(jnp.bfloat16)
        for c in halo_copies(l):
            c.start()

    copy_nodes.wait()
    send_halo(0)

    live = count[0]
    for k in range(E // CHUNK):
        rows = pl.ds(k * CHUNK, CHUNK)
        x[rows, pl.ds(LOC, NV + 2 * HALO)] = hot(column(snd, k), NV + 2 * HALO, 0)
        x[rows, pl.ds(REC, NV)] = hot(column(rcv, k), NV, 0)
        slot = lax.broadcasted_iota(jnp.int32, (NV, CHUNK), 1) + k * CHUNK
        node = lax.broadcasted_iota(jnp.int32, (NV, CHUNK), 0)
        row = jnp.broadcast_to(rcv[k : k + 1, :], (NV, CHUNK))
        oht[:, rows] = jnp.where((row == node) & (slot < live), 1.0, 0.0).astype(jnp.bfloat16)

    copy_edges.wait()

    def arrived(l, p, ref):
        pltpu.make_async_copy(ref, ref, w_sem.at[l, p]).wait()

    def layer(l, carry):
        sec = l // OWN
        sub = lax.rem(l, OWN)

        @pl.when(sub == 0)
        def _():
            arrived(sec, 5, egs.at[sec])
            arrived(sec, 6, ngs.at[sec])

        arrived(l, 0, w23.at[l])
        wcat[l, pl.ds(D, NV), :] = dot(nodes[...], w23[l, pl.ds(D, D), :]).astype(jnp.bfloat16)
        wcat[l, pl.ds(LOC, NV), :] = dot(nodes[...], w23[l, pl.ds(0, D), :]).astype(jnp.bfloat16)
        arrived(l, 1, wcat.at[l, pl.ds(0, D)])
        for t in range(E // TILE):
            rows = pl.ds(t * TILE, TILE)
            pre[rows, :] = dot(x[rows, pl.ds(0, HAL)], wcat[l, pl.ds(0, HAL), :])
        arrived(l, 3, ni.at[l])
        pre_node[...] = dot(nodes[...], ni[l, pl.ds(0, D), :])

        for c in halo_copies(l):
            c.wait_recv()
        wcat[l, pl.ds(HAL, 2 * HALO), :] = dot(halo[l], w23[l, pl.ds(0, D), :]).astype(jnp.bfloat16)
        arrived(l, 2, wo.at[l])
        gain = egs[sec, pl.ds(sub, 1), :]
        for t in range(E // TILE):
            rows = pl.ds(t * TILE, TILE)
            full = pre[rows, :] + dot(x[rows, pl.ds(HAL, 2 * HALO)], wcat[l, pl.ds(HAL, 2 * HALO), :])
            update = dot(silu(full).astype(jnp.bfloat16), wo[l])
            x[rows, pl.ds(0, D)] = residual_norm(x[rows, pl.ds(0, D)], update, gain)
        aggregate = dot(oht[...], x[:, pl.ds(0, D)]).astype(jnp.bfloat16)

        arrived(l, 4, no.at[l])
        hidden = silu(pre_node[...] + dot(aggregate, ni[l, pl.ds(D, D), :])).astype(jnp.bfloat16)
        nodes[...] = residual_norm(nodes[...], dot(hidden, no[l]), ngs[sec, pl.ds(sub, 1), :])

        @pl.when(l < L - 1)
        def _():
            send_halo(l + 1)

        return carry

    lax.fori_loop(0, L, layer, 0)
    out[0] = nodes[...]

    for c in remote:
        c.wait_send()
    for l in range(L):
        for c in halo_copies(l):
            c.wait_send()


def on_device(node_latents, edge_latents, sender, receiver, send_up, send_down, edge_count, wei, weo, eg, wni, wno, ng):
    n_node = lax.axis_size("node")
    vmem = pl.BlockSpec(memory_space=pltpu.VMEM)
    smem = pl.BlockSpec(memory_space=pltpu.SMEM)
    hbm = pl.BlockSpec(memory_space=pl.ANY)
    bf16, f32 = jnp.bfloat16, jnp.float32
    return pl.pallas_call(
        functools.partial(kernel, n_node),
        out_shape=jax.ShapeDtypeStruct((1, NV, D), bf16),
        in_specs=[hbm, hbm, vmem, vmem, vmem, vmem, smem, hbm, hbm, hbm, hbm, hbm, hbm],
        out_specs=vmem,
        scratch_shapes=[
            pltpu.VMEM((NV, D), bf16),
            pltpu.VMEM((E, XW), bf16),
            pltpu.VMEM((E, D), f32),
            pltpu.VMEM((NV, E), bf16),
            pltpu.VMEM((2 * HALO, NV), bf16),
            pltpu.VMEM((L, XW, D), bf16),
            pltpu.VMEM((L, 2 * D, D), bf16),
            pltpu.VMEM((L, D, D), bf16),
            pltpu.VMEM((L, 2 * D, D), bf16),
            pltpu.VMEM((L, D, D), bf16),
            pltpu.VMEM((2, OWN, D), f32),
            pltpu.VMEM((2, OWN, D), f32),
            pltpu.VMEM((L, 2 * HALO, D), bf16),
            pltpu.VMEM((L, 2 * HALO, D), bf16),
            pltpu.VMEM((NV, D), f32),
            pltpu.SemaphoreType.DMA((2,)),
            pltpu.SemaphoreType.DMA((L, 7)),
            pltpu.SemaphoreType.DMA((OWN, 7)),
            pltpu.SemaphoreType.DMA((L, 2)),
            pltpu.SemaphoreType.DMA((L, 2)),
        ],
        compiler_params=pltpu.CompilerParams(
            collective_id=0, has_side_effects=True, vmem_limit_bytes=56 * 1024 * 1024
        ),
        cost_estimate=pl.CostEstimate(
            flops=2 * L * 5 * E * D * D, bytes_accessed=18 * 1024 * 1024, transcendentals=L * E * D
        ),
    )(
        node_latents,
        edge_latents,
        sender.reshape(E // CHUNK, CHUNK),
        receiver.reshape(E // CHUNK, CHUNK),
        send_up.reshape(1, HALO),
        send_down.reshape(1, HALO),
        edge_count,
        wei,
        weo,
        eg,
        wni,
        wno,
        ng,
    )


def solution(mesh):
    return jax.shard_map(
        on_device,
        mesh=mesh,
        in_specs=(
            P(None, "node", None),
            P(None, "node", None),
            P("node"),
            P("node"),
            P("node"),
            P("node"),
            P("node"),
            P("section", None, None),
            P("section", None, None),
            P("section", None),
            P("section", None, None),
            P("section", None, None),
            P("section", None),
        ),
        out_specs=P("section", "node", None),
        check_vma=False,
    )
```

```python
import functools

import jax
import jax.numpy as jnp
from jax import lax
from jax.experimental import pallas as pl
from jax.experimental.pallas import tpu as pltpu
from jax.sharding import PartitionSpec as P

D = 512
NV = 256
HALO = 128
E = 1536
L = 4
OWN = 2
TILE = 256
BTILE = 256
CHUNK = 128
MESH = pl.DeviceIdType.MESH

REC = D
LOC = REC + NV
HAL = LOC + NV
XW = HAL + 2 * HALO


def silu_of_half(half):
    return (half + half * jnp.tanh(half)).astype(jnp.bfloat16)


def centred(weight):
    weight = weight.astype(jnp.float32)
    return (weight - jnp.mean(weight, axis=-1, keepdims=True)).astype(jnp.bfloat16)


def residual_norm(base, update, gain):
    scale = lax.rsqrt(jnp.mean(update * update, axis=-1, keepdims=True) + 1e-05)
    return (base.astype(jnp.float32) + (update * scale) * gain).astype(jnp.bfloat16)


def halved(value):
    return (0.5 * value.astype(jnp.float32)).astype(jnp.bfloat16)


def dot(a, b):
    return jnp.dot(a, b, preferred_element_type=jnp.float32)


def kernel(
    n_node,
    node_in,
    edge_in,
    snd_in,
    rcv_in,
    up_in,
    dn_in,
    count_in,
    wei,
    weo,
    eg,
    wni,
    wno,
    ng,
    out,
    snd,
    rcv,
    upw,
    dnw,
    count,
    nodes,
    x,
    pre,
    hid,
    oht,
    pick,
    wcat,
    w23,
    wo,
    ni,
    no,
    egs,
    ngs,
    halo,
    sendbuf,
    pre_node,
    in_sem,
    w_sem,
    ws_sem,
    h_recv,
    h_send,
):
    me = lax.axis_index("section")
    other = 1 - me
    at = lax.axis_index("node")
    above = lax.rem(at + 1, n_node)
    below = lax.rem(at + n_node - 1, n_node)

    copy_nodes = pltpu.make_async_copy(node_in.at[me], nodes, in_sem.at[0])
    copy_picks = [
        pltpu.make_async_copy(up_in, upw, in_sem.at[2]),
        pltpu.make_async_copy(dn_in, dnw, in_sem.at[3]),
    ]
    copy_ends = [
        pltpu.make_async_copy(snd_in, snd, in_sem.at[4]),
        pltpu.make_async_copy(rcv_in, rcv, in_sem.at[5]),
        pltpu.make_async_copy(count_in, count, in_sem.at[6]),
    ]
    for c in copy_picks + [copy_nodes] + copy_ends:
        c.start()

    def pieces(j):
        k = OWN * me + j
        return [
            (wei.at[j, pl.ds(D, 2 * D)], w23.at[k]),
            (wei.at[j, pl.ds(0, D)], wcat.at[k, pl.ds(0, D)]),
            (weo.at[j], wo.at[k]),
            (wni.at[j], ni.at[k]),
            (wno.at[j], no.at[k]),
        ]

    own = []
    for j in range(OWN):
        for p, (src, dst) in enumerate(pieces(j)):
            own.append(pltpu.make_async_copy(src, dst, w_sem.at[OWN * me + j, p]))
    own.append(pltpu.make_async_copy(eg, egs.at[me], w_sem.at[me, 5]))
    own.append(pltpu.make_async_copy(ng, ngs.at[me], w_sem.at[me, 6]))
    first = own[:5] + own[10:]
    for c in first[:2]:
        c.start()
    copy_edges = pltpu.make_async_copy(edge_in.at[me], x.at[:, pl.ds(0, D)], in_sem.at[1])
    copy_edges.start()
    for c in first[2:]:
        c.start()

    barrier = pltpu.get_barrier_semaphore()
    for target in ({"section": other}, {"node": above}, {"node": below}):
        pl.semaphore_signal(barrier, inc=1, device_id=target, device_id_type=MESH)

    remote = []
    for j in range(OWN):
        for p, (src, dst) in enumerate(pieces(j)):
            remote.append((src, dst, ws_sem.at[j, p], w_sem.at[OWN * me + j, p]))
    remote.insert(3, (eg, egs.at[me], ws_sem.at[0, 5], w_sem.at[me, 5]))
    remote.insert(4, (ng, ngs.at[me], ws_sem.at[0, 6], w_sem.at[me, 6]))
    remote = [
        pltpu.make_async_remote_copy(
            src_ref=s, dst_ref=d, send_sem=a, recv_sem=b, device_id={"section": other}, device_id_type=MESH
        )
        for s, d, a, b in remote
    ]

    def column(ref, k):
        return jnp.broadcast_to(ref[k : k + 1, :], (CHUNK, CHUNK)).T

    def hot(col, width, base):
        rows = col.shape[0]
        parts = []
        for q in range(width // CHUNK):
            lanes = lax.broadcasted_iota(jnp.int32, (rows, CHUNK), 1) + (base + q * CHUNK)
            parts.append(jnp.where(col == lanes, 1.0, 0.0).astype(jnp.bfloat16))
        return jnp.concatenate(parts, axis=1)

    for c in copy_picks:
        c.wait()
    pick[pl.ds(0, HALO), :] = hot(column(upw, 0), NV, 0)
    pick[pl.ds(HALO, HALO), :] = hot(column(dnw, 0), NV, 0)

    def halo_copies(l):
        return [
            pltpu.make_async_remote_copy(
                src_ref=sendbuf.at[l, pl.ds(q * HALO, HALO)],
                dst_ref=halo.at[l, pl.ds(q * HALO, HALO)],
                send_sem=h_send.at[l, q],
                recv_sem=h_recv.at[l, q],
                device_id={"node": target},
                device_id_type=MESH,
            )
            for q, target in enumerate((above, below))
        ]

    def send_halo(l):
        sendbuf[l] = dot(pick[...], nodes[...]).astype(jnp.bfloat16)
        for c in halo_copies(l):
            c.start()

    copy_nodes.wait()
    sendbuf[0] = dot(pick[...], nodes[...]).astype(jnp.bfloat16)
    pl.semaphore_wait(barrier, 3)
    for c in halo_copies(0) + remote[:7]:
        c.start()

    for c in copy_ends:
        c.wait()
    live = count[0]
    for k in range(E // CHUNK):
        rows = pl.ds(k * CHUNK, CHUNK)
        x[rows, pl.ds(LOC, NV + 2 * HALO)] = hot(column(snd, k), NV + 2 * HALO, 0)
        x[rows, pl.ds(REC, NV)] = hot(column(rcv, k), NV, 0)
        slot = lax.broadcasted_iota(jnp.int32, (NV, CHUNK), 1) + k * CHUNK
        node = lax.broadcasted_iota(jnp.int32, (NV, CHUNK), 0)
        row = jnp.broadcast_to(rcv[k : k + 1, :], (NV, CHUNK))
        oht[:, rows] = jnp.where((row == node) & (slot < live), 1.0, 0.0).astype(jnp.bfloat16)

    for c in own[5:10] + remote[7:]:
        c.start()
    copy_edges.wait()

    def arrived(l, p, ref):
        pltpu.make_async_copy(ref, ref, w_sem.at[l, p]).wait()

    def layer(l, carry):
        sec = l // OWN
        sub = lax.rem(l, OWN)

        @pl.when(sub == 0)
        def _():
            arrived(sec, 5, egs.at[sec])
            arrived(sec, 6, ngs.at[sec])

        arrived(l, 0, w23.at[l])
        wcat[l, pl.ds(D, NV), :] = halved(dot(nodes[...], w23[l, pl.ds(D, D), :]))
        wcat[l, pl.ds(LOC, NV), :] = halved(dot(nodes[...], w23[l, pl.ds(0, D), :]))
        arrived(l, 1, wcat.at[l, pl.ds(0, D)])
        wcat[l, pl.ds(0, D), :] = halved(wcat[l, pl.ds(0, D), :])
        for t in range(E // TILE):
            rows = pl.ds(t * TILE, TILE)
            pre[rows, :] = dot(x[rows, pl.ds(0, HAL)], wcat[l, pl.ds(0, HAL), :])
        arrived(l, 2, wo.at[l])
        wo[l] = centred(wo[l])
        arrived(l, 3, ni.at[l])
        ni[l] = halved(ni[l])
        arrived(l, 4, no.at[l])
        no[l] = centred(no[l])
        pre_node[...] = dot(nodes[...], ni[l, pl.ds(0, D), :])

        for c in halo_copies(l):
            c.wait_recv()
        wcat[l, pl.ds(HAL, 2 * HALO), :] = halved(dot(halo[l], w23[l, pl.ds(0, D), :]))
        gain = egs[sec, pl.ds(sub, 1), :]
        tiles = [pl.ds(t * BTILE, BTILE) for t in range(E // BTILE)]

        def stage1(rows):
            full = pre[rows, :] + dot(x[rows, pl.ds(HAL, 2 * HALO)], wcat[l, pl.ds(HAL, 2 * HALO), :])
            hid[rows, :] = silu_of_half(full)

        def stage2(rows):
            pre[rows, :] = dot(hid[rows, :], wo[l])

        def stage3(rows):
            x[rows, pl.ds(0, D)] = residual_norm(x[rows, pl.ds(0, D)], pre[rows, :], gain)

        stages = (stage1, stage2, stage3)
        for step in range(len(tiles) + len(stages) - 1):
            for k, stage in enumerate(stages):
                if 0 <= step - k < len(tiles):
                    stage(tiles[step - k])
        aggregate = dot(oht[...], x[:, pl.ds(0, D)]).astype(jnp.bfloat16)

        hidden = silu_of_half(pre_node[...] + dot(aggregate, ni[l, pl.ds(D, D), :]))
        nodes[...] = residual_norm(nodes[...], dot(hidden, no[l]), ngs[sec, pl.ds(sub, 1), :])

        @pl.when(l < L - 1)
        def _():
            send_halo(l + 1)

        return carry

    lax.fori_loop(0, L, layer, 0)
    out[0] = nodes[...]

    for c in remote:
        c.wait_send()
    for l in range(L):
        for c in halo_copies(l):
            c.wait_send()


def on_device(node_latents, edge_latents, sender, receiver, send_up, send_down, edge_count, wei, weo, eg, wni, wno, ng):
    n_node = lax.axis_size("node")
    vmem = pl.BlockSpec(memory_space=pltpu.VMEM)
    hbm = pl.BlockSpec(memory_space=pl.ANY)
    bf16, f32 = jnp.bfloat16, jnp.float32
    return pl.pallas_call(
        functools.partial(kernel, n_node),
        out_shape=jax.ShapeDtypeStruct((1, NV, D), bf16),
        in_specs=[hbm, hbm, hbm, hbm, hbm, hbm, hbm, hbm, hbm, hbm, hbm, hbm, hbm],
        out_specs=vmem,
        scratch_shapes=[
            pltpu.VMEM((E // CHUNK, CHUNK), jnp.int32),
            pltpu.VMEM((E // CHUNK, CHUNK), jnp.int32),
            pltpu.VMEM((1, HALO), jnp.int32),
            pltpu.VMEM((1, HALO), jnp.int32),
            pltpu.SMEM((1,), jnp.int32),
            pltpu.VMEM((NV, D), bf16),
            pltpu.VMEM((E, XW), bf16),
            pltpu.VMEM((E, D), f32),
            pltpu.VMEM((E, D), bf16),
            pltpu.VMEM((NV, E), bf16),
            pltpu.VMEM((2 * HALO, NV), bf16),
            pltpu.VMEM((L, XW, D), bf16),
            pltpu.VMEM((L, 2 * D, D), bf16),
            pltpu.VMEM((L, D, D), bf16),
            pltpu.VMEM((L, 2 * D, D), bf16),
            pltpu.VMEM((L, D, D), bf16),
            pltpu.VMEM((2, OWN, D), f32),
            pltpu.VMEM((2, OWN, D), f32),
            pltpu.VMEM((L, 2 * HALO, D), bf16),
            pltpu.VMEM((L, 2 * HALO, D), bf16),
            pltpu.VMEM((NV, D), f32),
            pltpu.SemaphoreType.DMA((7,)),
            pltpu.SemaphoreType.DMA((L, 7)),
            pltpu.SemaphoreType.DMA((OWN, 7)),
            pltpu.SemaphoreType.DMA((L, 2)),
            pltpu.SemaphoreType.DMA((L, 2)),
        ],
        compiler_params=pltpu.CompilerParams(
            collective_id=0, has_side_effects=True, vmem_limit_bytes=56 * 1024 * 1024
        ),
        cost_estimate=pl.CostEstimate(
            flops=2 * L * 5 * E * D * D, bytes_accessed=18 * 1024 * 1024, transcendentals=L * E * D
        ),
    )(
        node_latents,
        edge_latents,
        sender.reshape(E // CHUNK, CHUNK),
        receiver.reshape(E // CHUNK, CHUNK),
        send_up.reshape(1, HALO),
        send_down.reshape(1, HALO),
        edge_count,
        wei,
        weo,
        eg,
        wni,
        wno,
        ng,
    )


def solution(mesh):
    return jax.shard_map(
        on_device,
        mesh=mesh,
        in_specs=(
            P(None, "node", None),
            P(None, "node", None),
            P("node"),
            P("node"),
            P("node"),
            P("node"),
            P("node"),
            P("section", None, None),
            P("section", None, None),
            P("section", None),
            P("section", None, None),
            P("section", None, None),
            P("section", None),
        ),
        out_specs=P("section", "node", None),
        check_vma=False,
    )
```

```python
import functools

import jax
import jax.numpy as jnp
from jax import lax
from jax.experimental import pallas as pl
from jax.experimental.pallas import tpu as pltpu
from jax.sharding import PartitionSpec as P

D = 512
NV = 256
HALO = 128
E = 1536
L = 4
OWN = 2
TILE = 256
BTILE = 256
CHUNK = 128
MESH = pl.DeviceIdType.MESH

REC = D
LOC = REC + NV
HAL = LOC + NV
XW = HAL + 2 * HALO


def silu_of_half(half):
    return (half + half * jnp.tanh(half)).astype(jnp.bfloat16)


def centred(weight):
    weight = weight.astype(jnp.float32)
    return (weight - jnp.mean(weight, axis=-1, keepdims=True)).astype(jnp.bfloat16)


def residual_norm(base, update, gain):
    scale = lax.rsqrt(jnp.mean(update * update, axis=-1, keepdims=True) + 1e-05)
    return (base.astype(jnp.float32) + (update * scale) * gain).astype(jnp.bfloat16)


def halved(value):
    return (0.5 * value.astype(jnp.float32)).astype(jnp.bfloat16)


def dot(a, b):
    return jnp.dot(a, b, preferred_element_type=jnp.float32)


def kernel(
    n_node,
    node_in,
    edge_in,
    snd_in,
    rcv_in,
    up_in,
    dn_in,
    count_in,
    wei,
    weo,
    eg,
    wni,
    wno,
    ng,
    out,
    snd,
    rcv,
    upw,
    dnw,
    count,
    nodes,
    x,
    pre,
    hid,
    oht,
    pick,
    wcat,
    w23,
    wo,
    ni,
    no,
    egs,
    ngs,
    halo,
    sendbuf,
    pre_node,
    in_sem,
    w_sem,
    ws_sem,
    h_recv,
    h_send,
):
    me = lax.axis_index("section")
    other = 1 - me
    at = lax.axis_index("node")
    above = lax.rem(at + 1, n_node)
    below = lax.rem(at + n_node - 1, n_node)

    barrier = pltpu.get_barrier_semaphore()
    for target in ({"section": other}, {"node": above}, {"node": below}):
        pl.semaphore_signal(barrier, inc=1, device_id=target, device_id_type=MESH)

    copy_nodes = pltpu.make_async_copy(node_in.at[me], nodes, in_sem.at[0])
    copy_picks = [
        pltpu.make_async_copy(up_in, upw, in_sem.at[2]),
        pltpu.make_async_copy(dn_in, dnw, in_sem.at[3]),
    ]
    copy_ends = [
        pltpu.make_async_copy(snd_in, snd, in_sem.at[4]),
        pltpu.make_async_copy(rcv_in, rcv, in_sem.at[5]),
        pltpu.make_async_copy(count_in, count, in_sem.at[6]),
    ]
    for c in copy_picks + [copy_nodes] + copy_ends:
        c.start()

    def pieces(j):
        k = OWN * me + j
        return [
            (wei.at[j, pl.ds(D, 2 * D)], w23.at[k]),
            (wei.at[j, pl.ds(0, D)], wcat.at[k, pl.ds(0, D)]),
            (weo.at[j], wo.at[k]),
            (wni.at[j], ni.at[k]),
            (wno.at[j], no.at[k]),
        ]

    own = []
    for j in range(OWN):
        for p, (src, dst) in enumerate(pieces(j)):
            own.append(pltpu.make_async_copy(src, dst, w_sem.at[OWN * me + j, p]))
    own.append(pltpu.make_async_copy(eg, egs.at[me], w_sem.at[me, 5]))
    own.append(pltpu.make_async_copy(ng, ngs.at[me], w_sem.at[me, 6]))
    first = own[:5] + own[10:]
    for c in first[:2]:
        c.start()
    copy_edges = pltpu.make_async_copy(edge_in.at[me], x.at[:, pl.ds(0, D)], in_sem.at[1])
    copy_edges.start()
    for c in first[2:]:
        c.start()


    remote = []
    for j in range(OWN):
        for p, (src, dst) in enumerate(pieces(j)):
            remote.append((src, dst, ws_sem.at[j, p], w_sem.at[OWN * me + j, p]))
    remote.insert(3, (eg, egs.at[me], ws_sem.at[0, 5], w_sem.at[me, 5]))
    remote.insert(4, (ng, ngs.at[me], ws_sem.at[0, 6], w_sem.at[me, 6]))
    remote = [
        pltpu.make_async_remote_copy(
            src_ref=s, dst_ref=d, send_sem=a, recv_sem=b, device_id={"section": other}, device_id_type=MESH
        )
        for s, d, a, b in remote
    ]

    def column(ref, k):
        return jnp.broadcast_to(ref[k : k + 1, :], (CHUNK, CHUNK)).T

    def hot(col, width, base):
        rows = col.shape[0]
        parts = []
        for q in range(width // CHUNK):
            lanes = lax.broadcasted_iota(jnp.int32, (rows, CHUNK), 1) + (base + q * CHUNK)
            parts.append(jnp.where(col == lanes, 1.0, 0.0).astype(jnp.bfloat16))
        return jnp.concatenate(parts, axis=1)

    for c in copy_picks:
        c.wait()
    pick[pl.ds(0, HALO), :] = hot(column(upw, 0), NV, 0)
    pick[pl.ds(HALO, HALO), :] = hot(column(dnw, 0), NV, 0)

    def halo_copies(l):
        return [
            pltpu.make_async_remote_copy(
                src_ref=sendbuf.at[l, pl.ds(q * HALO, HALO)],
                dst_ref=halo.at[l, pl.ds(q * HALO, HALO)],
                send_sem=h_send.at[l, q],
                recv_sem=h_recv.at[l, q],
                device_id={"node": target},
                device_id_type=MESH,
            )
            for q, target in enumerate((above, below))
        ]

    def send_halo(l):
        sendbuf[l] = dot(pick[...], nodes[...]).astype(jnp.bfloat16)
        for c in halo_copies(l):
            c.start()

    copy_nodes.wait()
    sendbuf[0] = dot(pick[...], nodes[...]).astype(jnp.bfloat16)
    pl.semaphore_wait(barrier, 3)
    for c in halo_copies(0) + remote[:7]:
        c.start()

    for c in copy_ends:
        c.wait()
    live = count[0]
    for k in range(E // CHUNK):
        rows = pl.ds(k * CHUNK, CHUNK)
        x[rows, pl.ds(LOC, NV + 2 * HALO)] = hot(column(snd, k), NV + 2 * HALO, 0)
        x[rows, pl.ds(REC, NV)] = hot(column(rcv, k), NV, 0)
        slot = lax.broadcasted_iota(jnp.int32, (NV, CHUNK), 1) + k * CHUNK
        node = lax.broadcasted_iota(jnp.int32, (NV, CHUNK), 0)
        row = jnp.broadcast_to(rcv[k : k + 1, :], (NV, CHUNK))
        oht[:, rows] = jnp.where((row == node) & (slot < live), 1.0, 0.0).astype(jnp.bfloat16)

    for c in own[5:10] + remote[7:]:
        c.start()
    copy_edges.wait()

    def arrived(l, p, ref):
        pltpu.make_async_copy(ref, ref, w_sem.at[l, p]).wait()

    def layer(l, carry):
        sec = l // OWN
        sub = lax.rem(l, OWN)

        @pl.when(sub == 0)
        def _():
            arrived(sec, 5, egs.at[sec])
            arrived(sec, 6, ngs.at[sec])

        arrived(l, 0, w23.at[l])
        wcat[l, pl.ds(D, NV), :] = halved(dot(nodes[...], w23[l, pl.ds(D, D), :]))
        wcat[l, pl.ds(LOC, NV), :] = halved(dot(nodes[...], w23[l, pl.ds(0, D), :]))
        arrived(l, 1, wcat.at[l, pl.ds(0, D)])
        wcat[l, pl.ds(0, D), :] = halved(wcat[l, pl.ds(0, D), :])
        for t in range(E // TILE):
            rows = pl.ds(t * TILE, TILE)
            pre[rows, :] = dot(x[rows, pl.ds(0, HAL)], wcat[l, pl.ds(0, HAL), :])
        arrived(l, 2, wo.at[l])
        wo[l] = centred(wo[l])
        arrived(l, 3, ni.at[l])
        ni[l] = halved(ni[l])
        arrived(l, 4, no.at[l])
        no[l] = centred(no[l])
        pre_node[...] = dot(nodes[...], ni[l, pl.ds(0, D), :])

        for c in halo_copies(l):
            c.wait_recv()
        wcat[l, pl.ds(HAL, 2 * HALO), :] = halved(dot(halo[l], w23[l, pl.ds(0, D), :]))
        gain = egs[sec, pl.ds(sub, 1), :]
        tiles = [pl.ds(t * BTILE, BTILE) for t in range(E // BTILE)]

        def stage1(rows):
            full = pre[rows, :] + dot(x[rows, pl.ds(HAL, 2 * HALO)], wcat[l, pl.ds(HAL, 2 * HALO), :])
            hid[rows, :] = silu_of_half(full)

        def stage2(rows):
            pre[rows, :] = dot(hid[rows, :], wo[l])

        def stage3(rows):
            x[rows, pl.ds(0, D)] = residual_norm(x[rows, pl.ds(0, D)], pre[rows, :], gain)

        stages = (stage1, stage2, stage3)
        for step in range(len(tiles) + len(stages) - 1):
            for k, stage in enumerate(stages):
                if 0 <= step - k < len(tiles):
                    stage(tiles[step - k])
        aggregate = dot(oht[...], x[:, pl.ds(0, D)]).astype(jnp.bfloat16)

        hidden = silu_of_half(pre_node[...] + dot(aggregate, ni[l, pl.ds(D, D), :]))
        nodes[...] = residual_norm(nodes[...], dot(hidden, no[l]), ngs[sec, pl.ds(sub, 1), :])

        @pl.when(l < L - 1)
        def _():
            send_halo(l + 1)

        return carry

    lax.fori_loop(0, L, layer, 0)
    out[0] = nodes[...]

    for c in remote:
        c.wait_send()
    for l in range(L):
        for c in halo_copies(l):
            c.wait_send()


def on_device(node_latents, edge_latents, sender, receiver, send_up, send_down, edge_count, wei, weo, eg, wni, wno, ng):
    n_node = lax.axis_size("node")
    vmem = pl.BlockSpec(memory_space=pltpu.VMEM)
    hbm = pl.BlockSpec(memory_space=pl.ANY)
    bf16, f32 = jnp.bfloat16, jnp.float32
    return pl.pallas_call(
        functools.partial(kernel, n_node),
        out_shape=pltpu.VMEM((1, NV, D), bf16),
        in_specs=[hbm, hbm, hbm, hbm, hbm, hbm, hbm, hbm, hbm, hbm, hbm, hbm, hbm],
        out_specs=vmem,
        scratch_shapes=[
            pltpu.VMEM((E // CHUNK, CHUNK), jnp.int32),
            pltpu.VMEM((E // CHUNK, CHUNK), jnp.int32),
            pltpu.VMEM((1, HALO), jnp.int32),
            pltpu.VMEM((1, HALO), jnp.int32),
            pltpu.SMEM((1,), jnp.int32),
            pltpu.VMEM((NV, D), bf16),
            pltpu.VMEM((E, XW), bf16),
            pltpu.VMEM((E, D), f32),
            pltpu.VMEM((E, D), bf16),
            pltpu.VMEM((NV, E), bf16),
            pltpu.VMEM((2 * HALO, NV), bf16),
            pltpu.VMEM((L, XW, D), bf16),
            pltpu.VMEM((L, 2 * D, D), bf16),
            pltpu.VMEM((L, D, D), bf16),
            pltpu.VMEM((L, 2 * D, D), bf16),
            pltpu.VMEM((L, D, D), bf16),
            pltpu.VMEM((2, OWN, D), f32),
            pltpu.VMEM((2, OWN, D), f32),
            pltpu.VMEM((L, 2 * HALO, D), bf16),
            pltpu.VMEM((L, 2 * HALO, D), bf16),
            pltpu.VMEM((NV, D), f32),
            pltpu.SemaphoreType.DMA((7,)),
            pltpu.SemaphoreType.DMA((L, 7)),
            pltpu.SemaphoreType.DMA((OWN, 7)),
            pltpu.SemaphoreType.DMA((L, 2)),
            pltpu.SemaphoreType.DMA((L, 2)),
        ],
        compiler_params=pltpu.CompilerParams(
            collective_id=0, has_side_effects=True, vmem_limit_bytes=56 * 1024 * 1024
        ),
        cost_estimate=pl.CostEstimate(
            flops=2 * L * 5 * E * D * D, bytes_accessed=18 * 1024 * 1024, transcendentals=L * E * D
        ),
    )(
        node_latents,
        edge_latents,
        sender.reshape(E // CHUNK, CHUNK),
        receiver.reshape(E // CHUNK, CHUNK),
        send_up.reshape(1, HALO),
        send_down.reshape(1, HALO),
        edge_count,
        wei,
        weo,
        eg,
        wni,
        wno,
        ng,
    )


def solution(mesh):
    return jax.shard_map(
        on_device,
        mesh=mesh,
        in_specs=(
            P(None, "node", None),
            P(None, "node", None),
            P("node"),
            P("node"),
            P("node"),
            P("node"),
            P("node"),
            P("section", None, None),
            P("section", None, None),
            P("section", None),
            P("section", None, None),
            P("section", None, None),
            P("section", None),
        ),
        out_specs=P("section", "node", None),
        check_vma=False,
    )
```

```python
import functools

import jax
import jax.numpy as jnp
from jax import lax
from jax.experimental import pallas as pl
from jax.experimental.pallas import tpu as pltpu
from jax.sharding import PartitionSpec as P

D = 512
NV = 256
HALO = 128
E = 1536
L = 4
OWN = 2
TILE = 256
BTILE = 256
CHUNK = 128
PART = HALO // 2
MESH = pl.DeviceIdType.MESH

REC = D
LOC = REC + NV
HAL = LOC + NV
XW = HAL + 2 * HALO


def silu_of_half(half):
    return (half + half * jnp.tanh(half)).astype(jnp.bfloat16)


def centred(weight):
    weight = weight.astype(jnp.float32)
    return (weight - jnp.mean(weight, axis=-1, keepdims=True)).astype(jnp.bfloat16)


def residual_norm(base, update, gain):
    scale = lax.rsqrt(jnp.mean(update * update, axis=-1, keepdims=True) + 1e-05)
    return (base.astype(jnp.float32) + (update * scale) * gain).astype(jnp.bfloat16)


def halved(value):
    return (0.5 * value.astype(jnp.float32)).astype(jnp.bfloat16)


def dot(a, b):
    return jnp.dot(a, b, preferred_element_type=jnp.float32)


def kernel(
    n_node,
    node_in,
    edge_in,
    snd_in,
    rcv_in,
    up_in,
    dn_in,
    count_in,
    wei,
    weo,
    eg,
    wni,
    wno,
    ng,
    out,
    snd,
    rcv,
    upw,
    dnw,
    count,
    nodes,
    x,
    pre,
    hid,
    oht,
    ohts,
    pick,
    wcat,
    w23,
    wo,
    ni,
    no,
    egs,
    ngs,
    halo,
    sendbuf,
    pre_node,
    pre_sent,
    in_sem,
    w_sem,
    ws_sem,
    h_recv,
    h_send,
):
    me = lax.axis_index("section")
    other = 1 - me
    at = lax.axis_index("node")
    above = lax.rem(at + 1, n_node)
    below = lax.rem(at + n_node - 1, n_node)

    barrier = pltpu.get_barrier_semaphore()
    for target in ({"section": other}, {"node": above}, {"node": below}):
        pl.semaphore_signal(barrier, inc=1, device_id=target, device_id_type=MESH)

    copy_nodes = pltpu.make_async_copy(node_in.at[me], nodes, in_sem.at[0])
    copy_picks = [
        pltpu.make_async_copy(up_in, upw, in_sem.at[2]),
        pltpu.make_async_copy(dn_in, dnw, in_sem.at[3]),
    ]
    copy_ends = [
        pltpu.make_async_copy(snd_in, snd, in_sem.at[4]),
        pltpu.make_async_copy(rcv_in, rcv, in_sem.at[5]),
        pltpu.make_async_copy(count_in, count, in_sem.at[6]),
    ]
    for c in copy_picks + [copy_nodes] + copy_ends:
        c.start()

    def pieces(j):
        k = OWN * me + j
        return [
            (wei.at[j, pl.ds(D, 2 * D)], w23.at[k]),
            (wei.at[j, pl.ds(0, D)], wcat.at[k, pl.ds(0, D)]),
            (weo.at[j], wo.at[k]),
            (wni.at[j], ni.at[k]),
            (wno.at[j], no.at[k]),
        ]

    own = []
    for j in range(OWN):
        for p, (src, dst) in enumerate(pieces(j)):
            own.append(pltpu.make_async_copy(src, dst, w_sem.at[OWN * me + j, p]))
    own.append(pltpu.make_async_copy(eg, egs.at[me], w_sem.at[me, 5]))
    own.append(pltpu.make_async_copy(ng, ngs.at[me], w_sem.at[me, 6]))
    first = own[:5] + own[10:]
    for c in first[:2]:
        c.start()
    copy_edges = pltpu.make_async_copy(edge_in.at[me], x.at[:, pl.ds(0, D)], in_sem.at[1])
    copy_edges.start()
    for c in first[2:]:
        c.start()


    remote = []
    for j in range(OWN):
        for p, (src, dst) in enumerate(pieces(j)):
            remote.append((src, dst, ws_sem.at[j, p], w_sem.at[OWN * me + j, p]))
    remote.insert(3, (eg, egs.at[me], ws_sem.at[0, 5], w_sem.at[me, 5]))
    remote.insert(4, (ng, ngs.at[me], ws_sem.at[0, 6], w_sem.at[me, 6]))
    remote = [
        pltpu.make_async_remote_copy(
            src_ref=s, dst_ref=d, send_sem=a, recv_sem=b, device_id={"section": other}, device_id_type=MESH
        )
        for s, d, a, b in remote
    ]

    def column(ref, k):
        return jnp.broadcast_to(ref[k : k + 1, :], (CHUNK, CHUNK)).T

    def hot(col, width, base):
        rows = col.shape[0]
        parts = []
        for q in range(width // CHUNK):
            lanes = lax.broadcasted_iota(jnp.int32, (rows, CHUNK), 1) + (base + q * CHUNK)
            parts.append(jnp.where(col == lanes, 1.0, 0.0).astype(jnp.bfloat16))
        return jnp.concatenate(parts, axis=1)

    for c in copy_picks:
        c.wait()
    sent_up, sent_down = column(upw, 0), column(dnw, 0)
    sent = [jnp.concatenate([c[h * PART : (h + 1) * PART] for c in (sent_up, sent_down)], axis=0) for h in range(2)]
    for h in range(2):
        pick[pl.ds(h * HALO, HALO), :] = hot(sent[h], NV, 0)

    def halo_copies(l, h):
        return [
            pltpu.make_async_remote_copy(
                src_ref=sendbuf.at[l, pl.ds((2 * h + q) * PART, PART)],
                dst_ref=halo.at[l, pl.ds(q * HALO + h * PART, PART)],
                send_sem=h_send.at[l, h, q],
                recv_sem=h_recv.at[l, h, q],
                device_id={"node": target},
                device_id_type=MESH,
            )
            for q, target in enumerate((above, below))
        ]

    def all_halo_copies(l):
        return halo_copies(l, 0) + halo_copies(l, 1)

    copy_nodes.wait()
    sendbuf[0] = dot(pick[...], nodes[...]).astype(jnp.bfloat16)
    pl.semaphore_wait(barrier, 3)
    for c in all_halo_copies(0) + remote[:7]:
        c.start()

    for c in copy_ends:
        c.wait()
    live = count[0]
    for k in range(E // CHUNK):
        rows = pl.ds(k * CHUNK, CHUNK)
        x[rows, pl.ds(LOC, NV + 2 * HALO)] = hot(column(snd, k), NV + 2 * HALO, 0)
        x[rows, pl.ds(REC, NV)] = hot(column(rcv, k), NV, 0)
        slot = lax.broadcasted_iota(jnp.int32, (NV, CHUNK), 1) + k * CHUNK
        node = lax.broadcasted_iota(jnp.int32, (NV, CHUNK), 0)
        row = jnp.broadcast_to(rcv[k : k + 1, :], (NV, CHUNK))
        oht[:, rows] = jnp.where((row == node) & (slot < live), 1.0, 0.0).astype(jnp.bfloat16)
        for h in range(2):
            ohts[pl.ds(h * HALO, HALO), rows] = jnp.where(
                (row[:HALO] == sent[h]) & (slot[:HALO] < live), 1.0, 0.0
            ).astype(jnp.bfloat16)

    for c in own[5:10] + remote[7:]:
        c.start()
    copy_edges.wait()

    def arrived(l, p, ref):
        pltpu.make_async_copy(ref, ref, w_sem.at[l, p]).wait()

    def layer(l, last):
        sec = l // OWN
        sub = l % OWN

        if not last:

            @pl.when(sub == 0)
            def _():
                arrived(sec, 5, egs.at[sec])
                arrived(sec, 6, ngs.at[sec])

        arrived(l, 0, w23.at[l])
        wcat[l, pl.ds(D, NV), :] = halved(dot(nodes[...], w23[l, pl.ds(D, D), :]))
        wcat[l, pl.ds(LOC, NV), :] = halved(dot(nodes[...], w23[l, pl.ds(0, D), :]))
        arrived(l, 1, wcat.at[l, pl.ds(0, D)])
        wcat[l, pl.ds(0, D), :] = halved(wcat[l, pl.ds(0, D), :])
        for t in range(E // TILE):
            rows = pl.ds(t * TILE, TILE)
            pre[rows, :] = dot(x[rows, pl.ds(0, HAL)], wcat[l, pl.ds(0, HAL), :])
        arrived(l, 2, wo.at[l])
        wo[l] = centred(wo[l])
        arrived(l, 3, ni.at[l])
        ni[l] = halved(ni[l])
        arrived(l, 4, no.at[l])
        no[l] = centred(no[l])
        pre_node[...] = dot(nodes[...], ni[l, pl.ds(0, D), :])
        if not last:
            pre_sent[...] = dot(sendbuf[l], ni[l, pl.ds(0, D), :])

        for c in all_halo_copies(l):
            c.wait_recv()
        wcat[l, pl.ds(HAL, 2 * HALO), :] = halved(dot(halo[l], w23[l, pl.ds(0, D), :]))
        gain = egs[sec, pl.ds(sub, 1), :]
        tiles = [pl.ds(t * BTILE, BTILE) for t in range(E // BTILE)]

        def stage1(rows):
            full = pre[rows, :] + dot(x[rows, pl.ds(HAL, 2 * HALO)], wcat[l, pl.ds(HAL, 2 * HALO), :])
            hid[rows, :] = silu_of_half(full)

        def stage2(rows):
            pre[rows, :] = dot(hid[rows, :], wo[l])

        def stage3(rows):
            x[rows, pl.ds(0, D)] = residual_norm(x[rows, pl.ds(0, D)], pre[rows, :], gain)

        stages = (stage1, stage2, stage3)
        for step in range(len(tiles) + len(stages) - 1):
            for k, stage in enumerate(stages):
                if 0 <= step - k < len(tiles):
                    stage(tiles[step - k])
        node_gain = ngs[sec, pl.ds(sub, 1), :]

        def hidden_of(aggregate, pre_act):
            return silu_of_half(pre_act + dot(aggregate, ni[l, pl.ds(D, D), :]))

        if not last:
            aggregate = dot(ohts[...], x[:, pl.ds(0, D)]).astype(jnp.bfloat16)
            parts = [pl.ds(h * HALO, HALO) for h in range(2)]
            hidden = [hidden_of(aggregate[h * HALO : (h + 1) * HALO], pre_sent[parts[h], :]) for h in range(2)]
            for h in range(2):
                new = residual_norm(sendbuf[l, parts[h], :], dot(hidden[h], no[l]), node_gain)
                sendbuf[l + 1, parts[h], :] = new
                for c in halo_copies(l + 1, h):
                    c.start()

        aggregate = dot(oht[...], x[:, pl.ds(0, D)]).astype(jnp.bfloat16)
        hidden = hidden_of(aggregate, pre_node[...])
        nodes[...] = residual_norm(nodes[...], dot(hidden, no[l]), node_gain)

    def step(l, carry):
        layer(l, False)
        return carry

    lax.fori_loop(0, L - 1, step, 0)
    layer(L - 1, True)
    out[0] = nodes[...]

    for c in remote:
        c.wait_send()
    for l in range(L):
        for c in all_halo_copies(l):
            c.wait_send()


def on_device(node_latents, edge_latents, sender, receiver, send_up, send_down, edge_count, wei, weo, eg, wni, wno, ng):
    n_node = lax.axis_size("node")
    vmem = pl.BlockSpec(memory_space=pltpu.VMEM)
    hbm = pl.BlockSpec(memory_space=pl.ANY)
    bf16, f32 = jnp.bfloat16, jnp.float32
    return pl.pallas_call(
        functools.partial(kernel, n_node),
        out_shape=pltpu.VMEM((1, NV, D), bf16),
        in_specs=[hbm, hbm, hbm, hbm, hbm, hbm, hbm, hbm, hbm, hbm, hbm, hbm, hbm],
        out_specs=vmem,
        scratch_shapes=[
            pltpu.VMEM((E // CHUNK, CHUNK), jnp.int32),
            pltpu.VMEM((E // CHUNK, CHUNK), jnp.int32),
            pltpu.VMEM((1, HALO), jnp.int32),
            pltpu.VMEM((1, HALO), jnp.int32),
            pltpu.SMEM((1,), jnp.int32),
            pltpu.VMEM((NV, D), bf16),
            pltpu.VMEM((E, XW), bf16),
            pltpu.VMEM((E, D), f32),
            pltpu.VMEM((E, D), bf16),
            pltpu.VMEM((NV, E), bf16),
            pltpu.VMEM((2 * HALO, E), bf16),
            pltpu.VMEM((2 * HALO, NV), bf16),
            pltpu.VMEM((L, XW, D), bf16),
            pltpu.VMEM((L, 2 * D, D), bf16),
            pltpu.VMEM((L, D, D), bf16),
            pltpu.VMEM((L, 2 * D, D), bf16),
            pltpu.VMEM((L, D, D), bf16),
            pltpu.VMEM((2, OWN, D), f32),
            pltpu.VMEM((2, OWN, D), f32),
            pltpu.VMEM((L, 2 * HALO, D), bf16),
            pltpu.VMEM((L, 2 * HALO, D), bf16),
            pltpu.VMEM((NV, D), f32),
            pltpu.VMEM((2 * HALO, D), f32),
            pltpu.SemaphoreType.DMA((7,)),
            pltpu.SemaphoreType.DMA((L, 7)),
            pltpu.SemaphoreType.DMA((OWN, 7)),
            pltpu.SemaphoreType.DMA((L, 2, 2)),
            pltpu.SemaphoreType.DMA((L, 2, 2)),
        ],
        compiler_params=pltpu.CompilerParams(
            collective_id=0, has_side_effects=True, vmem_limit_bytes=56 * 1024 * 1024
        ),
        cost_estimate=pl.CostEstimate(
            flops=2 * L * 5 * E * D * D, bytes_accessed=18 * 1024 * 1024, transcendentals=L * E * D
        ),
    )(
        node_latents,
        edge_latents,
        sender.reshape(E // CHUNK, CHUNK),
        receiver.reshape(E // CHUNK, CHUNK),
        send_up.reshape(1, HALO),
        send_down.reshape(1, HALO),
        edge_count,
        wei,
        weo,
        eg,
        wni,
        wno,
        ng,
    )


def solution(mesh):
    return jax.shard_map(
        on_device,
        mesh=mesh,
        in_specs=(
            P(None, "node", None),
            P(None, "node", None),
            P("node"),
            P("node"),
            P("node"),
            P("node"),
            P("node"),
            P("section", None, None),
            P("section", None, None),
            P("section", None),
            P("section", None, None),
            P("section", None, None),
            P("section", None),
        ),
        out_specs=P("section", "node", None),
        check_vma=False,
    )
```

```python
import functools

import jax
import jax.numpy as jnp
from jax import lax
from jax.experimental import pallas as pl
from jax.experimental.pallas import tpu as pltpu
from jax.sharding import PartitionSpec as P

D = 512
NV = 256
HALO = 128
E = 1536
L = 4
OWN = 2
TILE = 256
BTILE = 256
CHUNK = 128
PART = HALO // 2
MESH = pl.DeviceIdType.MESH

REC = D
LOC = REC + NV
HAL = LOC + NV
XW = HAL + 2 * HALO


def silu_of_half(half):
    return (half + half * jnp.tanh(half)).astype(jnp.bfloat16)


def centred(weight):
    weight = weight.astype(jnp.float32)
    return (weight - jnp.mean(weight, axis=-1, keepdims=True)).astype(jnp.bfloat16)


def residual_norm(base, update, gain):
    scale = lax.rsqrt(jnp.mean(update * update, axis=-1, keepdims=True) + 1e-05)
    return (base.astype(jnp.float32) + (update * scale) * gain).astype(jnp.bfloat16)


def halved(value):
    return (0.5 * value.astype(jnp.float32)).astype(jnp.bfloat16)


def dot(a, b):
    return jnp.dot(a, b, preferred_element_type=jnp.float32)


def kernel(
    n_node,
    node_in,
    edge_in,
    snd_in,
    rcv_in,
    up_in,
    dn_in,
    count_in,
    wei,
    weo,
    eg,
    wni,
    wno,
    ng,
    out,
    snd,
    rcv,
    upw,
    dnw,
    count,
    nodes,
    x,
    pre,
    hid,
    oht,
    ohts,
    pick,
    wcat,
    w23,
    wo,
    ni,
    no,
    egs,
    ngs,
    halo,
    sendbuf,
    nodes_cross,
    crossbuf,
    pre_node,
    pre_sent,
    in_sem,
    w_sem,
    ws_sem,
    h_recv,
    h_send,
):
    me = lax.axis_index("section")
    other = 1 - me
    at = lax.axis_index("node")
    above = lax.rem(at + 1, n_node)
    below = lax.rem(at + n_node - 1, n_node)

    barrier = pltpu.get_barrier_semaphore()
    targets = [{"section": other}] + [{"section": c, "node": n} for c in (me, other) for n in (above, below)]
    for target in targets:
        pl.semaphore_signal(barrier, inc=1, device_id=target, device_id_type=MESH)

    copy_nodes = pltpu.make_async_copy(node_in.at[me], nodes, in_sem.at[0])
    copy_picks = [
        pltpu.make_async_copy(up_in, upw, in_sem.at[2]),
        pltpu.make_async_copy(dn_in, dnw, in_sem.at[3]),
    ]
    copy_ends = [
        pltpu.make_async_copy(snd_in, snd, in_sem.at[4]),
        pltpu.make_async_copy(rcv_in, rcv, in_sem.at[5]),
        pltpu.make_async_copy(count_in, count, in_sem.at[6]),
    ]
    copy_cross = pltpu.make_async_copy(node_in.at[other], nodes_cross, in_sem.at[7])
    for c in copy_picks + [copy_cross, copy_nodes] + copy_ends:
        c.start()

    def pieces(j):
        k = OWN * me + j
        return [
            (wei.at[j, pl.ds(D, 2 * D)], w23.at[k]),
            (wei.at[j, pl.ds(0, D)], wcat.at[k, pl.ds(0, D)]),
            (weo.at[j], wo.at[k]),
            (wni.at[j], ni.at[k]),
            (wno.at[j], no.at[k]),
        ]

    own = []
    for j in range(OWN):
        for p, (src, dst) in enumerate(pieces(j)):
            own.append(pltpu.make_async_copy(src, dst, w_sem.at[OWN * me + j, p]))
    own.append(pltpu.make_async_copy(eg, egs.at[me], w_sem.at[me, 5]))
    own.append(pltpu.make_async_copy(ng, ngs.at[me], w_sem.at[me, 6]))
    first = own[:5] + own[10:]
    for c in first[:2]:
        c.start()
    copy_edges = pltpu.make_async_copy(edge_in.at[me], x.at[:, pl.ds(0, D)], in_sem.at[1])
    copy_edges.start()
    for c in first[2:]:
        c.start()


    remote = []
    for j in range(OWN):
        for p, (src, dst) in enumerate(pieces(j)):
            remote.append((src, dst, ws_sem.at[j, p], w_sem.at[OWN * me + j, p]))
    remote.insert(3, (eg, egs.at[me], ws_sem.at[0, 5], w_sem.at[me, 5]))
    remote.insert(4, (ng, ngs.at[me], ws_sem.at[0, 6], w_sem.at[me, 6]))
    remote = [
        pltpu.make_async_remote_copy(
            src_ref=s, dst_ref=d, send_sem=a, recv_sem=b, device_id={"section": other}, device_id_type=MESH
        )
        for s, d, a, b in remote
    ]

    def column(ref, k):
        return jnp.broadcast_to(ref[k : k + 1, :], (CHUNK, CHUNK)).T

    def hot(col, width, base):
        rows = col.shape[0]
        parts = []
        for q in range(width // CHUNK):
            lanes = lax.broadcasted_iota(jnp.int32, (rows, CHUNK), 1) + (base + q * CHUNK)
            parts.append(jnp.where(col == lanes, 1.0, 0.0).astype(jnp.bfloat16))
        return jnp.concatenate(parts, axis=1)

    for c in copy_picks:
        c.wait()
    sent_up, sent_down = column(upw, 0), column(dnw, 0)
    sent = [jnp.concatenate([c[h * PART : (h + 1) * PART] for c in (sent_up, sent_down)], axis=0) for h in range(2)]
    for h in range(2):
        pick[pl.ds(h * HALO, HALO), :] = hot(sent[h], NV, 0)

    def halo_copies(l, h):
        return [
            pltpu.make_async_remote_copy(
                src_ref=sendbuf.at[l, pl.ds((2 * h + q) * PART, PART)],
                dst_ref=halo.at[l, pl.ds(q * HALO + h * PART, PART)],
                send_sem=h_send.at[l, h, q],
                recv_sem=h_recv.at[l, h, q],
                device_id={"node": target},
                device_id_type=MESH,
            )
            for q, target in enumerate((above, below))
        ]

    def all_halo_copies(l):
        return halo_copies(l, 0) + halo_copies(l, 1)

    copy_cross.wait()
    crossbuf[...] = dot(pick[...], nodes_cross[...]).astype(jnp.bfloat16)
    pl.semaphore_wait(barrier, 5)
    cross = [
        pltpu.make_async_remote_copy(
            src_ref=crossbuf.at[pl.ds((2 * h + q) * PART, PART)],
            dst_ref=halo.at[0, pl.ds(q * HALO + h * PART, PART)],
            send_sem=h_send.at[0, h, q],
            recv_sem=h_recv.at[0, h, q],
            device_id={"section": other, "node": target},
            device_id_type=MESH,
        )
        for h in range(2)
        for q, target in enumerate((above, below))
    ]
    for c in cross + remote[:7]:
        c.start()
    copy_nodes.wait()
    sendbuf[0] = dot(pick[...], nodes[...]).astype(jnp.bfloat16)

    for c in copy_ends:
        c.wait()
    live = count[0]
    for k in range(E // CHUNK):
        rows = pl.ds(k * CHUNK, CHUNK)
        x[rows, pl.ds(LOC, NV + 2 * HALO)] = hot(column(snd, k), NV + 2 * HALO, 0)
        x[rows, pl.ds(REC, NV)] = hot(column(rcv, k), NV, 0)
        slot = lax.broadcasted_iota(jnp.int32, (NV, CHUNK), 1) + k * CHUNK
        node = lax.broadcasted_iota(jnp.int32, (NV, CHUNK), 0)
        row = jnp.broadcast_to(rcv[k : k + 1, :], (NV, CHUNK))
        oht[:, rows] = jnp.where((row == node) & (slot < live), 1.0, 0.0).astype(jnp.bfloat16)
        for h in range(2):
            ohts[pl.ds(h * HALO, HALO), rows] = jnp.where(
                (row[:HALO] == sent[h]) & (slot[:HALO] < live), 1.0, 0.0
            ).astype(jnp.bfloat16)

    for c in own[5:10] + remote[7:]:
        c.start()
    copy_edges.wait()

    def arrived(l, p, ref):
        pltpu.make_async_copy(ref, ref, w_sem.at[l, p]).wait()

    def layer(l, last):
        sec = l // OWN
        sub = l % OWN

        if not last:

            @pl.when(sub == 0)
            def _():
                arrived(sec, 5, egs.at[sec])
                arrived(sec, 6, ngs.at[sec])

        arrived(l, 0, w23.at[l])
        wcat[l, pl.ds(D, NV), :] = halved(dot(nodes[...], w23[l, pl.ds(D, D), :]))
        wcat[l, pl.ds(LOC, NV), :] = halved(dot(nodes[...], w23[l, pl.ds(0, D), :]))
        arrived(l, 1, wcat.at[l, pl.ds(0, D)])
        wcat[l, pl.ds(0, D), :] = halved(wcat[l, pl.ds(0, D), :])
        for t in range(E // TILE):
            rows = pl.ds(t * TILE, TILE)
            pre[rows, :] = dot(x[rows, pl.ds(0, HAL)], wcat[l, pl.ds(0, HAL), :])
        arrived(l, 2, wo.at[l])
        wo[l] = centred(wo[l])
        arrived(l, 3, ni.at[l])
        ni[l] = halved(ni[l])
        arrived(l, 4, no.at[l])
        no[l] = centred(no[l])
        pre_node[...] = dot(nodes[...], ni[l, pl.ds(0, D), :])
        if not last:
            pre_sent[...] = dot(sendbuf[l], ni[l, pl.ds(0, D), :])

        for c in all_halo_copies(l):
            c.wait_recv()
        wcat[l, pl.ds(HAL, 2 * HALO), :] = halved(dot(halo[l], w23[l, pl.ds(0, D), :]))
        gain = egs[sec, pl.ds(sub, 1), :]
        tiles = [pl.ds(t * BTILE, BTILE) for t in range(E // BTILE)]

        def stage1(rows):
            full = pre[rows, :] + dot(x[rows, pl.ds(HAL, 2 * HALO)], wcat[l, pl.ds(HAL, 2 * HALO), :])
            hid[rows, :] = silu_of_half(full)

        def stage2(rows):
            pre[rows, :] = dot(hid[rows, :], wo[l])

        def stage3(rows):
            x[rows, pl.ds(0, D)] = residual_norm(x[rows, pl.ds(0, D)], pre[rows, :], gain)

        stages = (stage1, stage2, stage3)
        for step in range(len(tiles) + len(stages) - 1):
            for k, stage in enumerate(stages):
                if 0 <= step - k < len(tiles):
                    stage(tiles[step - k])
        node_gain = ngs[sec, pl.ds(sub, 1), :]

        def hidden_of(aggregate, pre_act):
            return silu_of_half(pre_act + dot(aggregate, ni[l, pl.ds(D, D), :]))

        if not last:
            aggregate = dot(ohts[...], x[:, pl.ds(0, D)]).astype(jnp.bfloat16)
            parts = [pl.ds(h * HALO, HALO) for h in range(2)]
            hidden = [hidden_of(aggregate[h * HALO : (h + 1) * HALO], pre_sent[parts[h], :]) for h in range(2)]
            for h in range(2):
                new = residual_norm(sendbuf[l, parts[h], :], dot(hidden[h], no[l]), node_gain)
                sendbuf[l + 1, parts[h], :] = new
                for c in halo_copies(l + 1, h):
                    c.start()

        aggregate = dot(oht[...], x[:, pl.ds(0, D)]).astype(jnp.bfloat16)
        hidden = hidden_of(aggregate, pre_node[...])
        nodes[...] = residual_norm(nodes[...], dot(hidden, no[l]), node_gain)

    def step(l, carry):
        layer(l, False)
        return carry

    lax.fori_loop(0, L - 1, step, 0)
    layer(L - 1, True)
    out[0] = nodes[...]

    for c in remote:
        c.wait_send()
    for l in range(L):
        for c in all_halo_copies(l):
            c.wait_send()


def on_device(node_latents, edge_latents, sender, receiver, send_up, send_down, edge_count, wei, weo, eg, wni, wno, ng):
    n_node = lax.axis_size("node")
    vmem = pl.BlockSpec(memory_space=pltpu.VMEM)
    hbm = pl.BlockSpec(memory_space=pl.ANY)
    bf16, f32 = jnp.bfloat16, jnp.float32
    return pl.pallas_call(
        functools.partial(kernel, n_node),
        out_shape=pltpu.VMEM((1, NV, D), bf16),
        in_specs=[hbm, hbm, hbm, hbm, hbm, hbm, hbm, hbm, hbm, hbm, hbm, hbm, hbm],
        out_specs=vmem,
        scratch_shapes=[
            pltpu.VMEM((E // CHUNK, CHUNK), jnp.int32),
            pltpu.VMEM((E // CHUNK, CHUNK), jnp.int32),
            pltpu.VMEM((1, HALO), jnp.int32),
            pltpu.VMEM((1, HALO), jnp.int32),
            pltpu.SMEM((1,), jnp.int32),
            pltpu.VMEM((NV, D), bf16),
            pltpu.VMEM((E, XW), bf16),
            pltpu.VMEM((E, D), f32),
            pltpu.VMEM((E, D), bf16),
            pltpu.VMEM((NV, E), bf16),
            pltpu.VMEM((2 * HALO, E), bf16),
            pltpu.VMEM((2 * HALO, NV), bf16),
            pltpu.VMEM((L, XW, D), bf16),
            pltpu.VMEM((L, 2 * D, D), bf16),
            pltpu.VMEM((L, D, D), bf16),
            pltpu.VMEM((L, 2 * D, D), bf16),
            pltpu.VMEM((L, D, D), bf16),
            pltpu.VMEM((2, OWN, D), f32),
            pltpu.VMEM((2, OWN, D), f32),
            pltpu.VMEM((L, 2 * HALO, D), bf16),
            pltpu.VMEM((L, 2 * HALO, D), bf16),
            pltpu.VMEM((NV, D), bf16),
            pltpu.VMEM((2 * HALO, D), bf16),
            pltpu.VMEM((NV, D), f32),
            pltpu.VMEM((2 * HALO, D), f32),
            pltpu.SemaphoreType.DMA((8,)),
            pltpu.SemaphoreType.DMA((L, 7)),
            pltpu.SemaphoreType.DMA((OWN, 7)),
            pltpu.SemaphoreType.DMA((L, 2, 2)),
            pltpu.SemaphoreType.DMA((L, 2, 2)),
        ],
        compiler_params=pltpu.CompilerParams(
            collective_id=0, has_side_effects=True, vmem_limit_bytes=56 * 1024 * 1024
        ),
        cost_estimate=pl.CostEstimate(
            flops=2 * L * 5 * E * D * D, bytes_accessed=18 * 1024 * 1024, transcendentals=L * E * D
        ),
    )(
        node_latents,
        edge_latents,
        sender.reshape(E // CHUNK, CHUNK),
        receiver.reshape(E // CHUNK, CHUNK),
        send_up.reshape(1, HALO),
        send_down.reshape(1, HALO),
        edge_count,
        wei,
        weo,
        eg,
        wni,
        wno,
        ng,
    )


def solution(mesh):
    return jax.shard_map(
        on_device,
        mesh=mesh,
        in_specs=(
            P(None, "node", None),
            P(None, "node", None),
            P("node"),
            P("node"),
            P("node"),
            P("node"),
            P("node"),
            P("section", None, None),
            P("section", None, None),
            P("section", None),
            P("section", None, None),
            P("section", None, None),
            P("section", None),
        ),
        out_specs=P("section", "node", None),
        check_vma=False,
    )
```
